256 devices in a mesh: rep: 16 (over z_hi, y), fsdp: 16 (over z_lo, x, core).
Axes of the slice: x: 4, y: 4, z: 8 (z_hi: 4, z_lo: 2; z = z_hi * 2 + z_lo), core: 2. Of those that a mesh axis runs over, the one named last changes fastest.
Arguments:
- query_states: bfloat16 [65536, 2048], P(('rep', 'fsdp')), may hold values from -6 to 6
- key_states: bfloat16 [65536, 1024], P(('rep', 'fsdp')), may hold values from -6 to 6
- value_states: bfloat16 [65536, 1024], P(('rep', 'fsdp')), may hold values from -6 to 6
- output_grad: bfloat16 [65536, 2304], P(('rep', 'fsdp')), may hold values from -6 to 6
- out_weight: bfloat16 [16, 2048, 2304], P('rep', 'fsdp'), may hold values from -0.125 to 0.125
- pseudo_grad: float32 [16, 2048, 2304], P('rep', 'fsdp'), may hold values from -6 to 6
- anchor: float32 [2048, 2304], P('fsdp'), may hold values from -6 to 6
- momentum: float32 [2048, 2304], P('fsdp', 'rep'), may hold values from -6 to 6
- local_weight: bfloat16 [16, 2048, 2304], P('rep', 'fsdp'), may hold values from -6 to 6
Outputs:
- branch_out: bfloat16 [65536, 2304], P(('rep', 'fsdp'))
- grad_q: bfloat16 [65536, 2048], P(('rep', 'fsdp'))
- grad_k: bfloat16 [65536, 1024], P(('rep', 'fsdp'))
- grad_v: bfloat16 [65536, 1024], P(('rep', 'fsdp'))
- weight_grad: bfloat16 [16, 2048, 2304], P('rep', 'fsdp')
- anchor_new: float32 [2048, 2304], P('fsdp')
- momentum_new: float32 [2048, 2304], P('fsdp', 'rep')
- merged: bfloat16 [16, 2048, 2304], P('rep', 'fsdp')
The draws below stay inside these ranges and needn't reach their ends.
All inputs are finite; a program needn't handle non-finite values.
Results may differ from the reference program's by a relative error of at most 0.022.
Values may be sent and summed in bfloat16 or wider, within the bound.
No kernel may reach another device: no remote copies, remote signals or barrier semaphores. Data moves between devices by JAX's collectives and lax.ppermute only.
A program may use at most 128 MiB of HBM per device.

```python
import jax
import jax.numpy as jnp
from jax import lax

DW = 2304
HEADS = 16
KV_HEADS = 8
HEAD_DIM = 128
TOK_DEV = 256
PROJ = 2048
REPLICAS = 16
TOKENS = 65536
N_REP = 16
N_FSDP = 16


def draw_query_states(key, part):
    key = jax.random.fold_in(key, 12)
    base = jnp.clip(jax.random.normal(key, (TOKENS, HEADS * HEAD_DIM), jnp.float32), -6.0, 6.0)
    return base.astype(jnp.bfloat16)


def draw_key_states(key, part):
    key = jax.random.fold_in(key, 21)
    base = jnp.clip(jax.random.normal(key, (TOKENS, KV_HEADS * HEAD_DIM), jnp.float32), -6.0, 6.0)
    return base.astype(jnp.bfloat16)


def block_scale(own_key, dims, split, low, high):
    loudness = 1.0
    for dim, parts in split:
        heights = jax.random.uniform(jax.random.fold_in(jax.random.fold_in(own_key, 6), dim), (parts,), jnp.float32, low / len(split), high / len(split))
        loudness = loudness * jnp.repeat(jnp.exp(heights), dims[dim] // parts).reshape((-1,) + (1,) * (len(dims) - 1 - dim))
    return loudness


def noise(rng, shape, scale, bound, cuts=(), held_as=jnp.bfloat16):
    loudness = block_scale(rng, shape, cuts, -0.22, 0.18) if cuts else 1.0
    array = jax.random.normal(rng, shape, jnp.float32) * scale * loudness
    return jnp.minimum(jnp.maximum(array, -bound), bound).astype(held_as)


def setup_inputs(seed: int = 0) -> dict:
    splits = jax.random.split(jax.random.key(seed), 10)
    return {
        "query_states": draw_query_states(jax.random.fold_in(splits[9], 71), 0),
        "key_states": draw_key_states(jax.random.fold_in(splits[9], 71), 0),
        "value_states": noise(splits[2], (TOKENS, KV_HEADS * HEAD_DIM), 1.0, 6.0, ((0, 256),)),
        "output_grad": noise(splits[3], (TOKENS, DW), 1.0, 6.0, ((0, 256),)),
        "out_weight": noise(splits[4], (REPLICAS, PROJ, DW), PROJ ** -0.5, 0.125, ((0, 16), (1, 16))),
        "pseudo_grad": noise(splits[5], (REPLICAS, PROJ, DW), 1.0, 6.0, ((0, 16), (1, 16)), jnp.float32),
        "anchor": noise(splits[6], (PROJ, DW), 1.0, 6.0, ((0, 16),), jnp.float32),
        "momentum": noise(splits[7], (PROJ, DW), 1.0, 6.0, ((0, 16), (1, 16)), jnp.float32),
        "local_weight": noise(splits[8], (REPLICAS, PROJ, DW), 1.0, 6.0, ((0, 16), (1, 16))),
    }


query_scale = 1.0 / 12.0
outer_rate = 0.7
outer_moment = 0.9
mix_factor = 0.5


def round_trip(tensor):
    return lax.optimization_barrier(tensor.astype(jnp.bfloat16)).astype(jnp.float32)


def split_heads(query_states, key_states, value_states):
    length = query_states.shape[0]
    per_group = HEADS // KV_HEADS
    query_heads = query_states.astype(jnp.float32).reshape(length, KV_HEADS, per_group, HEAD_DIM)
    key_heads = key_states.astype(jnp.float32).reshape(length, KV_HEADS, HEAD_DIM)
    value_heads = value_states.astype(jnp.float32).reshape(length, KV_HEADS, HEAD_DIM)
    return query_heads, key_heads, value_heads


def causal_softmax(query_heads, key_heads):
    length = query_heads.shape[0]
    scores = jnp.einsum("igrd,jgd->grij", query_heads, key_heads) * query_scale
    allowed = jnp.arange(length)[:, None] >= jnp.arange(length)[None, :]
    scores = jnp.where(allowed, scores, -jnp.inf)
    highest = jnp.max(scores, axis=-1, keepdims=True)
    exponent_terms = jnp.exp(scores - highest)
    return exponent_terms / jnp.sum(exponent_terms, axis=-1, keepdims=True)


def forward_block(blocks):
    query_heads, key_heads, value_heads = split_heads(*blocks)
    attention = causal_softmax(query_heads, key_heads)
    mixed_rows = jnp.einsum("grij,jgd->igrd", round_trip(attention), value_heads)
    return mixed_rows.reshape(query_heads.shape[0], PROJ).astype(jnp.bfloat16)


def backward_block(blocks):
    query_states, key_states, value_states, grad_mixed = blocks
    length = query_states.shape[0]
    per_group = HEADS // KV_HEADS
    query_heads, key_heads, value_heads = split_heads(query_states, key_states, value_states)
    attention = causal_softmax(query_heads, key_heads)
    grad_heads = grad_mixed.astype(jnp.float32).reshape(length, KV_HEADS, per_group, HEAD_DIM)
    grad_probs = jnp.einsum("igrd,jgd->grij", grad_heads, value_heads)
    row_term = jnp.sum(attention * grad_probs, axis=-1, keepdims=True)
    grad_scores = round_trip(attention * (grad_probs - row_term) * query_scale)
    grad_query = jnp.einsum("grij,jgd->igrd", grad_scores, key_heads).reshape(length, PROJ)
    grad_key = jnp.einsum("grij,igrd->jgd", grad_scores, query_heads).reshape(length, KV_HEADS * HEAD_DIM)
    grad_value = jnp.einsum("grij,igrd->jgd", round_trip(attention), grad_heads).reshape(length, KV_HEADS * HEAD_DIM)
    return grad_query.astype(jnp.bfloat16), grad_key.astype(jnp.bfloat16), grad_value.astype(jnp.bfloat16)


def replica_work(blocks):
    mixed_rows, grad_rows, weight_rows = blocks
    branch = jnp.dot(mixed_rows, weight_rows, preferred_element_type=jnp.float32).astype(jnp.bfloat16)
    grad_mixed = lax.dot_general(grad_rows, weight_rows, (((1,), (1,)), ((), ())), preferred_element_type=jnp.float32).astype(jnp.bfloat16)
    mixed_blocks = mixed_rows.astype(jnp.float32).reshape(N_FSDP, TOK_DEV, PROJ)
    grad_blocks = grad_rows.astype(jnp.float32).reshape(N_FSDP, TOK_DEV, DW)
    partials = round_trip(jnp.einsum("bsf,bsd->bfd", mixed_blocks, grad_blocks))
    weight_grad = jnp.sum(partials, axis=0).astype(jnp.bfloat16)
    return branch, grad_mixed, weight_grad


def reference(query_states, key_states, value_states, output_grad, out_weight, pseudo_grad, anchor, momentum, local_weight):
    sequences = TOKENS // TOK_DEV
    query_seq = query_states.reshape(sequences, TOK_DEV, PROJ)
    key_seq = key_states.reshape(sequences, TOK_DEV, KV_HEADS * HEAD_DIM)
    value_seq = value_states.reshape(sequences, TOK_DEV, KV_HEADS * HEAD_DIM)
    mixed_all = lax.map(forward_block, (query_seq, key_seq, value_seq))
    per_replica = N_FSDP * TOK_DEV
    branch, grad_mixed, weight_grad = lax.map(replica_work, (mixed_all.reshape(N_REP, per_replica, PROJ), output_grad.reshape(N_REP, per_replica, DW), out_weight))
    grad_query, grad_key, grad_value = lax.map(backward_block, (query_seq, key_seq, value_seq, grad_mixed.reshape(sequences, TOK_DEV, PROJ)))
    mean_delta = jnp.sum(pseudo_grad, axis=0) / N_REP
    momentum_new = outer_moment * momentum + mean_delta
    anchor_new = anchor - outer_rate * (outer_moment * momentum_new + mean_delta)
    merged = (mix_factor * local_weight.astype(jnp.float32) + mix_factor * anchor_new[None]).astype(jnp.bfloat16)
    return (branch.reshape(TOKENS, DW), grad_query.reshape(TOKENS, PROJ), grad_key.reshape(TOKENS, KV_HEADS * HEAD_DIM),
            grad_value.reshape(TOKENS, KV_HEADS * HEAD_DIM), weight_grad, anchor_new, momentum_new, merged)
```

```python
import jax
import jax.numpy as jnp
from jax import lax
from jax.sharding import PartitionSpec as P

HEADS = 16
KV_HEADS = 8
HEAD_DIM = 128


query_scale = 1.0 / 12.0
outer_rate = 0.7
outer_moment = 0.9
mix_factor = 0.5


def causal_softmax(query_heads, key_heads):
    length = query_heads.shape[0]
    scores = (
        jnp.einsum("igrd,jgd->grij", query_heads, key_heads, preferred_element_type=jnp.float32)
        * query_scale
    )
    allowed = jnp.arange(length)[:, None] >= jnp.arange(length)[None, :]
    scores = jnp.where(allowed, scores, -jnp.inf)
    highest = jnp.max(scores, axis=-1, keepdims=True)
    exponent_terms = jnp.exp(scores - highest)
    return exponent_terms / jnp.sum(exponent_terms, axis=-1, keepdims=True)


def on_device(
    query_states,
    key_states,
    value_states,
    output_grad,
    out_weight,
    pseudo_grad,
    anchor,
    momentum,
    local_weight,
):
    length = query_states.shape[0]
    per_group = HEADS // KV_HEADS
    query_heads = query_states.reshape(length, KV_HEADS, per_group, HEAD_DIM)
    key_heads = key_states.reshape(length, KV_HEADS, HEAD_DIM)
    value_heads = value_states.reshape(length, KV_HEADS, HEAD_DIM)
    attention = causal_softmax(query_heads, key_heads)
    attention_b = attention.astype(jnp.bfloat16)
    mixed_rows = jnp.einsum(
        "grij,jgd->igrd", attention_b, value_heads, preferred_element_type=jnp.float32
    )
    mixed_rows = mixed_rows.reshape(length, HEADS * HEAD_DIM).astype(jnp.bfloat16)
    own_rows = out_weight[0]
    full_weight = lax.all_gather(own_rows, "fsdp", axis=0, tiled=True)
    branch = jnp.dot(mixed_rows, full_weight, preferred_element_type=jnp.float32)
    grad_mixed = lax.dot_general(
        output_grad, full_weight, (((1,), (1,)), ((), ())), preferred_element_type=jnp.float32
    )
    branch_out = branch.astype(jnp.bfloat16)
    grad_mixed = grad_mixed.astype(jnp.bfloat16)
    weight_grad = lax.psum_scatter(
        lax.dot_general(
            mixed_rows, output_grad, (((0,), (0,)), ((), ())), preferred_element_type=jnp.float32
        ).astype(jnp.bfloat16),
        "fsdp",
        scatter_dimension=0,
        tiled=True,
    ).astype(jnp.float32)
    weight_grad = weight_grad.astype(jnp.bfloat16)[None]
    grad_heads = grad_mixed.reshape(length, KV_HEADS, per_group, HEAD_DIM)
    grad_probs = jnp.einsum(
        "igrd,jgd->grij", grad_heads, value_heads, preferred_element_type=jnp.float32
    )
    row_term = jnp.sum(attention * grad_probs, axis=-1, keepdims=True)
    grad_scores = (attention * (grad_probs - row_term) * query_scale).astype(jnp.bfloat16)
    grad_query = jnp.einsum(
        "grij,jgd->igrd", grad_scores, key_heads, preferred_element_type=jnp.float32
    )
    grad_key = jnp.einsum(
        "grij,igrd->jgd", grad_scores, query_heads, preferred_element_type=jnp.float32
    )
    grad_value = jnp.einsum(
        "grij,igrd->jgd", attention_b, grad_heads, preferred_element_type=jnp.float32
    )
    grad_query = grad_query.reshape(length, HEADS * HEAD_DIM).astype(jnp.bfloat16)
    grad_key = grad_key.reshape(length, KV_HEADS * HEAD_DIM).astype(jnp.bfloat16)
    grad_value = grad_value.reshape(length, KV_HEADS * HEAD_DIM).astype(jnp.bfloat16)
    replicas = lax.axis_size("rep")
    share_width = momentum.shape[1]
    own_delta = pseudo_grad[0]
    rows = own_delta.shape[0]
    shares = own_delta.astype(jnp.bfloat16).reshape(rows, replicas, share_width).transpose(1, 0, 2)
    shares = lax.all_to_all(shares, "rep", 0, 0, tiled=False)
    mean_share = jnp.sum(shares.astype(jnp.float32), axis=0) / replicas
    momentum_new = outer_moment * momentum + mean_share
    step_share = (outer_moment * momentum_new + mean_share).astype(jnp.bfloat16)
    steps = lax.all_to_all(
        jnp.broadcast_to(step_share[None], (replicas, rows, share_width)),
        "rep", 0, 0, tiled=False,
    )
    step_full = steps.transpose(1, 0, 2).reshape(rows, replicas * share_width)
    anchor_new = anchor - outer_rate * step_full.astype(jnp.float32)
    merged = (mix_factor * local_weight[0].astype(jnp.float32) + mix_factor * anchor_new).astype(
        jnp.bfloat16
    )[None]
    return (
        branch_out,
        grad_query,
        grad_key,
        grad_value,
        weight_grad,
        anchor_new,
        momentum_new,
        merged,
    )


def solution(mesh):
    return jax.shard_map(
        on_device,
        mesh=mesh,
        in_specs=(
            P(("rep", "fsdp"), None),
            P(("rep", "fsdp"), None),
            P(("rep", "fsdp"), None),
            P(("rep", "fsdp"), None),
            P("rep", "fsdp", None),
            P("rep", "fsdp", None),
            P("fsdp", None),
            P("fsdp", "rep"),
            P("rep", "fsdp", None),
        ),
        out_specs=(
            P(("rep", "fsdp"), None),
            P(("rep", "fsdp"), None),
            P(("rep", "fsdp"), None),
            P(("rep", "fsdp"), None),
            P("rep", "fsdp", None),
            P("fsdp", None),
            P("fsdp", "rep"),
            P("rep", "fsdp", None),
        ),
        check_vma=False,
    )
```

```python
import math

import jax
import jax.numpy as jnp
from jax import lax
from jax.experimental import pallas as pl
from jax.experimental.pallas import tpu as pltpu
from jax.sharding import PartitionSpec as P

HEADS = 16
KV_HEADS = 8
HEAD_DIM = 128

query_scale = 1.0 / 12.0
outer_rate = 0.7
outer_moment = 0.9
mix_factor = 0.5

X_SIZE = 4
Z_SIZE = 2
VMEM_LIMIT = 56 * 1024 * 1024

NT = (((1,), (1,)), ((), ()))
TN = (((0,), (0,)), ((), ()))


def f32_dot(left, right, dims=(((1,), (0,)), ((), ()))):
    return lax.dot_general(left, right, dims, preferred_element_type=jnp.float32)


def params(**kwargs):
    return pltpu.CompilerParams(vmem_limit_bytes=VMEM_LIMIT, **kwargs)


def cost(microseconds, bytes_accessed):
    return pl.CostEstimate(
        flops=int(microseconds * 1.15e9), bytes_accessed=bytes_accessed, transcendentals=0
    )


def own_lanes(place_ref, turn):
    parity = place_ref[KV_HEADS] if turn == 0 else 1 - place_ref[KV_HEADS]
    return pl.ds(pl.multiple_of(parity * HEAD_DIM, HEAD_DIM), HEAD_DIM)


def forward_kernel(place_ref, q_ref, k_ref, v_ref, own_ref, other_ref, attention_ref):
    length = q_ref.shape[0]
    keys, values = k_ref[...], v_ref[...]
    allowed = lax.broadcasted_iota(jnp.int32, (length, length), 0) >= lax.broadcasted_iota(
        jnp.int32, (length, length), 1
    )
    for turn, out_ref in enumerate((own_ref, other_ref)):
        scores = f32_dot(q_ref[:, own_lanes(place_ref, turn)], keys, NT)
        scores = jnp.where(allowed, scores, -jnp.inf)
        highest = jnp.max(scores, axis=-1, keepdims=True)
        terms = jnp.exp2((scores - highest) * (query_scale * math.log2(math.e)))
        attention = terms * (1.0 / jnp.sum(terms, axis=-1, keepdims=True))
        attention_ref[0, turn] = attention
        out_ref[...] = f32_dot(attention.astype(jnp.bfloat16), values).astype(jnp.bfloat16)


def forward(place, query_states, key_states, value_states):
    length = query_states.shape[0]
    pair = 2 * HEAD_DIM
    half = KV_HEADS * HEAD_DIM
    kv_spec = pl.BlockSpec((length, HEAD_DIM), lambda r, place: (0, place[r]))
    out_spec = pl.BlockSpec((length, HEAD_DIM), lambda r, place: (0, r))
    return pl.pallas_call(
        forward_kernel,
        grid_spec=pltpu.PrefetchScalarGridSpec(
            num_scalar_prefetch=1,
            grid=(KV_HEADS,),
            in_specs=[
                pl.BlockSpec((length, pair), lambda r, place: (0, place[r])),
                kv_spec,
                kv_spec,
            ],
            out_specs=[
                out_spec,
                out_spec,
                pl.BlockSpec((1, 2, length, length), lambda r, place: (r, 0, 0, 0)),
            ],
        ),
        out_shape=[
            jax.ShapeDtypeStruct((length, half), jnp.bfloat16),
            jax.ShapeDtypeStruct((length, half), jnp.bfloat16),
            jax.ShapeDtypeStruct((KV_HEADS, 2, length, length), jnp.float32),
        ],
        compiler_params=params(),
        cost_estimate=cost(9, 8 * 2**20),
        name="attention_forward",
    )(place, query_states, key_states, value_states)


def backward_kernel(
    place_ref, q_ref, k_ref, v_ref, attention_ref, own_ref, other_ref, dq_ref, dk_ref, dv_ref
):
    keys, values = k_ref[...], v_ref[...]
    for turn, grad_ref in enumerate((own_ref, other_ref)):
        lanes = own_lanes(place_ref, turn)
        grad_mixed = grad_ref[...]
        attention = attention_ref[0, turn]
        grad_probs = f32_dot(grad_mixed, values, NT)
        row_term = jnp.sum(attention * grad_probs, axis=-1, keepdims=True)
        grad_scores = (attention * (grad_probs - row_term) * query_scale).astype(jnp.bfloat16)
        dq_ref[:, lanes] = f32_dot(grad_scores, keys).astype(jnp.bfloat16)
        dk = f32_dot(grad_scores, q_ref[:, lanes], TN)
        dv = f32_dot(attention.astype(jnp.bfloat16), grad_mixed, TN)
        if turn == 0:
            dk_sum, dv_sum = dk, dv
    dk_ref[...] = (dk_sum + dk).astype(jnp.bfloat16)
    dv_ref[...] = (dv_sum + dv).astype(jnp.bfloat16)


def backward(place, query_states, key_states, value_states, attention, grad_own, grad_other):
    length = query_states.shape[0]
    pair = 2 * HEAD_DIM
    pair_spec = pl.BlockSpec((length, pair), lambda r, place: (0, place[r]))
    kv_spec = pl.BlockSpec((length, HEAD_DIM), lambda r, place: (0, place[r]))
    slot_spec = pl.BlockSpec((length, HEAD_DIM), lambda r, place: (0, r))
    return pl.pallas_call(
        backward_kernel,
        grid_spec=pltpu.PrefetchScalarGridSpec(
            num_scalar_prefetch=1,
            grid=(KV_HEADS,),
            in_specs=[
                pair_spec,
                kv_spec,
                kv_spec,
                pl.BlockSpec((1, 2, length, length), lambda r, place: (r, 0, 0, 0)),
                slot_spec,
                slot_spec,
            ],
            out_specs=[pair_spec, kv_spec, kv_spec],
        ),
        out_shape=[
            jax.ShapeDtypeStruct(query_states.shape, jnp.bfloat16),
            jax.ShapeDtypeStruct(key_states.shape, jnp.bfloat16),
            jax.ShapeDtypeStruct(value_states.shape, jnp.bfloat16),
        ],
        compiler_params=params(),
        cost_estimate=cost(10, 9 * 2**20),
        name="attention_backward",
    )(place, query_states, key_states, value_states, attention, grad_own, grad_other)


COLUMN_TILES = 3


def weight_grad_kernel(splits, m0_ref, m1_ref, g0_ref, g1_ref, *out_refs):
    product = f32_dot(m0_ref[...], g0_ref[...], TN) + f32_dot(m1_ref[...], g1_ref[...], TN)
    product = product.astype(jnp.bfloat16)
    start = 0
    for rows, out_ref in zip(splits, out_refs):
        out_ref[...] = product[start : start + rows]
        start += rows


def weight_grad_pieces(mixed_own, mixed_peer, grad_own, grad_peer, splits):
    length, half = mixed_own.shape
    width = grad_own.shape[1]
    tile = width // COLUMN_TILES
    whole = pl.BlockSpec((length, half), lambda j: (0, 0))
    part = pl.BlockSpec((length, tile), lambda j: (0, j))
    return pl.pallas_call(
        lambda *refs: weight_grad_kernel(splits, *refs),
        grid=(COLUMN_TILES,),
        in_specs=[whole, whole, part, part],
        out_specs=[pl.BlockSpec((rows, tile), lambda j: (0, j)) for rows in splits],
        out_shape=[jax.ShapeDtypeStruct((rows, width), jnp.bfloat16) for rows in splits],
        compiler_params=params(),
        cost_estimate=cost(5, 8 * 2**20),
        name="weight_grad_partial",
    )(mixed_own, mixed_peer, grad_own, grad_peer)


def grad_mixed_kernel(g0_ref, g1_ref, *refs):
    *pieces, out0_ref, out1_ref, sum0, sum1 = refs
    step = pl.program_id(0)
    weight = jnp.concatenate([piece[...] for piece in pieces], axis=0)
    part0 = f32_dot(g0_ref[...], weight, NT)
    part1 = f32_dot(g1_ref[...], weight, NT)

    @pl.when(step == 0)
    def _():
        sum0[...] = part0
        sum1[...] = part1

    @pl.when(step > 0)
    def _():
        sum0[...] += part0
        sum1[...] += part1

    @pl.when(step == COLUMN_TILES - 1)
    def _():
        out0_ref[...] = sum0[...].astype(jnp.bfloat16)
        out1_ref[...] = sum1[...].astype(jnp.bfloat16)


def grad_mixed_of(grad_own, grad_peer, pieces):
    length, width = grad_own.shape
    tile = width // COLUMN_TILES
    out_width = sum(piece.shape[0] for piece in pieces)
    part = pl.BlockSpec((length, tile), lambda j: (0, j))
    out_spec = pl.BlockSpec((length, out_width), lambda j: (0, 0))
    out = jax.ShapeDtypeStruct((length, out_width), jnp.bfloat16)
    return pl.pallas_call(
        grad_mixed_kernel,
        grid=(COLUMN_TILES,),
        in_specs=[part, part]
        + [pl.BlockSpec((piece.shape[0], tile), lambda j: (0, j)) for piece in pieces],
        out_specs=[out_spec, out_spec],
        out_shape=[out, out],
        scratch_shapes=[pltpu.VMEM((length, out_width), jnp.float32)] * 2,
        compiler_params=params(),
        cost_estimate=cost(6, 8 * 2**20),
        name="grad_mixed",
    )(grad_own, grad_peer, *pieces)


def branch_kernel(addends, mixed_ref, *refs):
    *pieces, out_ref = refs
    added, pieces = pieces[:addends], pieces[addends:]
    weight = jnp.concatenate([piece[...] for piece in pieces], axis=0)
    product = f32_dot(mixed_ref[...], weight)
    for ref in added:
        product = product + ref[...].astype(jnp.float32)
    out_ref[...] = product.astype(jnp.bfloat16)


def branch_part(mixed, pieces, *addends):
    length, half = mixed.shape
    width = pieces[0].shape[1]
    tile = width // COLUMN_TILES
    part = pl.BlockSpec((length, tile), lambda j: (0, j))
    return pl.pallas_call(
        lambda *refs: branch_kernel(len(addends), *refs),
        grid=(COLUMN_TILES,),
        in_specs=[pl.BlockSpec((length, half), lambda j: (0, 0))]
        + [part] * len(addends)
        + [pl.BlockSpec((piece.shape[0], tile), lambda j: (0, j)) for piece in pieces],
        out_specs=part,
        out_shape=jax.ShapeDtypeStruct((length, width), jnp.bfloat16),
        compiler_params=params(),
        cost_estimate=cost(5, 8 * 2**20),
        name="branch",
    )(mixed, *addends, *pieces)


def shift(dz, dx, dcore):
    pairs = []
    for z in range(Z_SIZE):
        for x in range(X_SIZE):
            for core in range(2):
                target = ((z + dz) % Z_SIZE) * X_SIZE + (x + dx) % X_SIZE
                pairs.append(((z * X_SIZE + x) * 2 + core, target * 2 + (core + dcore) % 2))
    return pairs


def to_right(array):
    return lax.ppermute(array, "fsdp", shift(0, 1, 0))


def to_left(array):
    return lax.ppermute(array, "fsdp", shift(0, -1, 0))


def to_far(array):
    return lax.ppermute(array, "fsdp", shift(1, 0, 0))


def to_peer(array):
    return lax.ppermute(array, "fsdp", shift(0, 0, 1))


def added(*terms):
    total = terms[0].astype(jnp.float32)
    for term in terms[1:]:
        total = total + term.astype(jnp.float32)
    return total.astype(jnp.bfloat16)


def place_table():
    position = lax.axis_index("fsdp")
    z, x, core = position // (2 * X_SIZE), (position // 2) % X_SIZE, position % 2
    slots = jnp.arange(KV_HEADS, dtype=jnp.int32)
    heads = ((z + slots // X_SIZE) % Z_SIZE) * X_SIZE + (x + slots % X_SIZE) % X_SIZE
    return jnp.concatenate([heads, core[None]]).astype(jnp.int32)


def outer_update(own_delta, anchor, momentum, local):
    replicas = lax.axis_size("rep")
    rows, share_width = momentum.shape
    shares = own_delta.astype(jnp.bfloat16).reshape(rows, replicas, share_width)
    shares = lax.all_to_all(shares.transpose(1, 2, 0), "rep", 0, 0, tiled=False)
    mean_share = jnp.sum(shares.astype(jnp.float32), axis=0).T / replicas
    momentum_new = outer_moment * momentum + mean_share
    step_share = (outer_moment * momentum_new + mean_share).astype(jnp.bfloat16).T
    steps = jnp.broadcast_to(step_share[None], (replicas, share_width, rows))
    steps = lax.all_to_all(steps, "rep", 0, 0, tiled=False)
    step_full = steps.reshape(replicas * share_width, rows).T
    anchor_new = anchor - outer_rate * step_full.astype(jnp.float32)
    merged = mix_factor * local.astype(jnp.float32) + mix_factor * anchor_new
    return momentum_new, anchor_new, merged.astype(jnp.bfloat16)


def on_device(
    query_states,
    key_states,
    value_states,
    output_grad,
    out_weight,
    pseudo_grad,
    anchor,
    momentum,
    local_weight,
):
    place = place_table()
    own_rows = out_weight[0]
    half = own_rows.shape[0] // 2
    grad_peer = to_peer(output_grad)

    w3 = to_right(own_rows)
    w1 = to_left(own_rows)
    w4 = to_far(own_rows)
    mixed_own, mixed_other, attention = forward(place, query_states, key_states, value_states)
    mixed_peer = to_peer(mixed_other)
    w1, w3, w4, mixed_own = lax.optimization_barrier((w1, w3, w4, mixed_own))
    w2a = to_right(w3[:half])
    w2b = to_left(w1[half:])
    w7 = to_right(w4)
    w5 = to_left(w4)

    rows = [2 * half, 2 * half, half, half, 2 * half, 2 * half, 2 * half, 2 * half, 2 * half]
    d0, d1, d2a, d2b, d3, d4, d5, d6, d7 = weight_grad_pieces(
        mixed_own, mixed_peer, output_grad, grad_peer, rows
    )
    w2a, w2b, d6 = lax.optimization_barrier((w2a, w2b, d6))
    w6a = to_far(w2a)
    w6b = to_far(w2b)
    pieces = [own_rows, w1, w2a, w2b, w3, w4, w5, w6a, w6b, w7]
    top, bottom = ((0, half), (0, 0)), ((half, 0), (0, 0))
    r2 = to_far(d6)
    r4l = to_left(d7)
    r4r = to_right(d5)
    from_far = to_far(added(d4, r4l, r4r))
    r3a = to_left(added(d2a, r2[:half]))
    r1b = to_right(added(d2b, r2[half:]))
    from_right = to_left(added(d3, jnp.pad(r3a, top)))
    from_left = to_right(added(d1, jnp.pad(r1b, bottom)))
    weight_grad = added(d0, from_right, from_left, from_far)[None]

    grad_mixed, grad_send = grad_mixed_of(output_grad, grad_peer, pieces)
    grad_mixed_other = to_peer(grad_send)
    branch_peer = to_peer(branch_part(mixed_peer, pieces))
    grad_query, grad_key, grad_value = backward(
        place, query_states, key_states, value_states, attention, grad_mixed, grad_mixed_other
    )
    branch_out = branch_part(mixed_own, pieces, branch_peer)

    momentum_new, anchor_new, merged = outer_update(
        pseudo_grad[0], anchor, momentum, local_weight[0]
    )
    return (
        branch_out,
        grad_query,
        grad_key,
        grad_value,
        weight_grad,
        anchor_new,
        momentum_new,
        merged[None],
    )


def solution(mesh):
    return jax.shard_map(
        on_device,
        mesh=mesh,
        in_specs=(
            P(("rep", "fsdp"), None),
            P(("rep", "fsdp"), None),
            P(("rep", "fsdp"), None),
            P(("rep", "fsdp"), None),
            P("rep", "fsdp", None),
            P("rep", "fsdp", None),
            P("fsdp", None),
            P("fsdp", "rep"),
            P("rep", "fsdp", None),
        ),
        out_specs=(
            P(("rep", "fsdp"), None),
            P(("rep", "fsdp"), None),
            P(("rep", "fsdp"), None),
            P(("rep", "fsdp"), None),
            P("rep", "fsdp", None),
            P("fsdp", None),
            P("fsdp", "rep"),
            P("rep", "fsdp", None),
        ),
        check_vma=False,
    )
```

```python
import math

import jax
import jax.numpy as jnp
from jax import lax
from jax.experimental import pallas as pl
from jax.experimental.pallas import tpu as pltpu
from jax.sharding import PartitionSpec as P

HEADS = 16
KV_HEADS = 8
HEAD_DIM = 128

query_scale = 1.0 / 12.0
outer_rate = 0.7
outer_moment = 0.9
mix_factor = 0.5

X_SIZE = 4
Z_SIZE = 2
VMEM_LIMIT = 56 * 1024 * 1024

NT = (((1,), (1,)), ((), ()))
TN = (((0,), (0,)), ((), ()))


def f32_dot(left, right, dims=(((1,), (0,)), ((), ()))):
    return lax.dot_general(left, right, dims, preferred_element_type=jnp.float32)


def params(**kwargs):
    return pltpu.CompilerParams(vmem_limit_bytes=VMEM_LIMIT, **kwargs)


def cost(microseconds, bytes_accessed):
    return pl.CostEstimate(
        flops=int(microseconds * 2.300e+07), bytes_accessed=bytes_accessed, transcendentals=0
    )


SLOT_Z = (0, 0, 0, 1, 1, 0, 1, 1)
SLOT_X = (0, 1, 3, 0, 1, 2, 3, 2)

ROW_BLOCKS = ((0, 128, 128), (128, 64, 256), (192, 64, 256))


def own_lanes(place_ref, turn):
    parity = place_ref[KV_HEADS] if turn == 0 else 1 - place_ref[KV_HEADS]
    return pl.ds(pl.multiple_of(parity * HEAD_DIM, HEAD_DIM), HEAD_DIM)


def both_heads(place_ref, ref):
    return jnp.concatenate([ref[:, own_lanes(place_ref, turn)] for turn in range(2)], axis=0)


def attention_of(scores):
    def block(turn, first, rows, seen):
        part = scores[pl.ds(turn * scores.shape[1] + first, rows), :seen]
        allowed = first + lax.broadcasted_iota(
            jnp.int32, (rows, seen), 0
        ) >= lax.broadcasted_iota(jnp.int32, (rows, seen), 1)
        part = jnp.where(allowed, part, -jnp.inf)
        highest = jnp.max(part, axis=-1, keepdims=True)
        terms = jnp.exp2((part - highest) * (query_scale * math.log2(math.e)))
        return terms * (1.0 / jnp.sum(terms, axis=-1, keepdims=True))

    return block


def put_rounded(ref, turn, first, rows, seen, values):
    length = ref.shape[1]
    stacked = pl.ds(turn * length + first, rows)
    ref[stacked, :seen] = values.astype(jnp.bfloat16)
    if seen < length:
        ref[stacked, seen:] = jnp.zeros((rows, length - seen), jnp.bfloat16)


def forward_kernel(place_ref, q_ref, k_ref, v_ref, own_ref, other_ref, scores_ref, rounded_ref):
    length = q_ref.shape[0]
    scores_ref[...] = f32_dot(both_heads(place_ref, q_ref), k_ref[...], NT)
    attention = attention_of(scores_ref)
    for turn in range(2):
        for block in ROW_BLOCKS:
            put_rounded(rounded_ref, turn, *block, attention(turn, *block))
    mixed = f32_dot(rounded_ref[...], v_ref[...]).astype(jnp.bfloat16)
    own_ref[...] = mixed[:length]
    other_ref[...] = mixed[length:]


def slot_specs(length):
    return (
        pl.BlockSpec((length, 2 * HEAD_DIM), lambda r, place: (0, place[r])),
        pl.BlockSpec((length, HEAD_DIM), lambda r, place: (0, place[r])),
        pl.BlockSpec((length, HEAD_DIM), lambda r, place: (0, r)),
    )


def forward(place, query_states, key_states, value_states):
    length = query_states.shape[0]
    pair_spec, kv_spec, slot_spec = slot_specs(length)
    out = jax.ShapeDtypeStruct((length, KV_HEADS * HEAD_DIM), jnp.bfloat16)
    return pl.pallas_call(
        forward_kernel,
        grid_spec=pltpu.PrefetchScalarGridSpec(
            num_scalar_prefetch=1,
            grid=(KV_HEADS,),
            in_specs=[pair_spec, kv_spec, kv_spec],
            out_specs=[slot_spec, slot_spec],
            scratch_shapes=[
                pltpu.VMEM((2 * length, length), jnp.float32),
                pltpu.VMEM((2 * length, length), jnp.bfloat16),
            ],
        ),
        out_shape=[out, out],
        compiler_params=params(),
        cost_estimate=cost(7, 4 * 2**20),
        name="attention_forward",
    )(place, query_states, key_states, value_states)


def backward_kernel(place_ref, q_ref, k_ref, v_ref, own_ref, other_ref, *refs):
    dq_ref, dk_ref, dv_ref, scores_ref, probs_ref, grad_scores_ref, rounded_ref = refs
    length = q_ref.shape[0]
    queries = both_heads(place_ref, q_ref)
    grad_mixed = jnp.concatenate([own_ref[...], other_ref[...]], axis=0)
    scores_ref[...] = f32_dot(queries, k_ref[...], NT)
    probs_ref[...] = f32_dot(grad_mixed, v_ref[...], NT)
    attention_block = attention_of(scores_ref)
    for turn in range(2):
        for block in ROW_BLOCKS:
            first, rows, seen = block
            attention = attention_block(turn, *block)
            grad_probs = probs_ref[pl.ds(turn * length + first, rows), :seen]
            row_term = jnp.sum(attention * grad_probs, axis=-1, keepdims=True)
            grad_scores = attention * (grad_probs - row_term) * query_scale
            put_rounded(grad_scores_ref, turn, *block, grad_scores)
            put_rounded(rounded_ref, turn, *block, attention)
    dv_ref[...] = f32_dot(rounded_ref[...], grad_mixed, TN).astype(jnp.bfloat16)
    dk_ref[...] = f32_dot(grad_scores_ref[...], queries, TN).astype(jnp.bfloat16)
    dq = f32_dot(grad_scores_ref[...], k_ref[...]).astype(jnp.bfloat16)
    for turn in range(2):
        dq_ref[:, own_lanes(place_ref, turn)] = dq[turn * length : (turn + 1) * length]


def backward(place, query_states, key_states, value_states, grad_own, grad_other):
    length = query_states.shape[0]
    pair_spec, kv_spec, slot_spec = slot_specs(length)
    return pl.pallas_call(
        backward_kernel,
        grid_spec=pltpu.PrefetchScalarGridSpec(
            num_scalar_prefetch=1,
            grid=(KV_HEADS,),
            in_specs=[pair_spec, kv_spec, kv_spec, slot_spec, slot_spec],
            out_specs=[pair_spec, kv_spec, kv_spec],
            scratch_shapes=[
                pltpu.VMEM((2 * length, length), jnp.float32),
                pltpu.VMEM((2 * length, length), jnp.float32),
                pltpu.VMEM((2 * length, length), jnp.bfloat16),
                pltpu.VMEM((2 * length, length), jnp.bfloat16),
            ],
        ),
        out_shape=[
            jax.ShapeDtypeStruct(query_states.shape, jnp.bfloat16),
            jax.ShapeDtypeStruct(key_states.shape, jnp.bfloat16),
            jax.ShapeDtypeStruct(value_states.shape, jnp.bfloat16),
        ],
        compiler_params=params(),
        cost_estimate=cost(10, 9 * 2**20),
        name="attention_backward",
    )(place, query_states, key_states, value_states, grad_own, grad_other)


COLUMN_TILES = 3


def weight_grad_kernel(m0_ref, m1_ref, g0_ref, g1_ref, *refs):
    *out_refs, mixed_ref = refs
    length = m0_ref.shape[0]

    @pl.when(pl.program_id(0) == 0)
    def _():
        mixed_ref[:, :length] = m0_ref[...].T
        mixed_ref[:, length:] = m1_ref[...].T

    grads = jnp.concatenate([g0_ref[...], g1_ref[...]], axis=0)
    product = f32_dot(mixed_ref[...], grads).astype(jnp.bfloat16)
    for slot, out_ref in enumerate(out_refs):
        out_ref[...] = product[slot * HEAD_DIM : (slot + 1) * HEAD_DIM]


def weight_grad_pieces(mixed_own, mixed_peer, grad_own, grad_peer):
    length, half = mixed_own.shape
    width = grad_own.shape[1]
    tile = width // COLUMN_TILES
    whole = pl.BlockSpec((length, half), lambda j: (0, 0))
    part = pl.BlockSpec((length, tile), lambda j: (0, j))
    return pl.pallas_call(
        weight_grad_kernel,
        grid=(COLUMN_TILES,),
        in_specs=[whole, whole, part, part],
        out_specs=[pl.BlockSpec((HEAD_DIM, tile), lambda j: (0, j))] * KV_HEADS,
        out_shape=[jax.ShapeDtypeStruct((HEAD_DIM, width), jnp.bfloat16)] * KV_HEADS,
        scratch_shapes=[pltpu.VMEM((half, 2 * length), jnp.bfloat16)],
        compiler_params=params(),
        cost_estimate=cost(5, 8 * 2**20),
        name="weight_grad_partial",
    )(mixed_own, mixed_peer, grad_own, grad_peer)


def project_kernel(g0_ref, g1_ref, m0_ref, m1_ref, *refs):
    *pieces, grad0_ref, grad1_ref, branch0_ref, branch1_ref, sum_ref = refs
    step = pl.program_id(0)
    length = g0_ref.shape[0]
    weight = jnp.concatenate([piece[...] for piece in pieces], axis=0)
    part = f32_dot(jnp.concatenate([g0_ref[...], g1_ref[...]], axis=0), weight, NT)

    @pl.when(step == 0)
    def _():
        sum_ref[...] = part

    @pl.when((step > 0) & (step < COLUMN_TILES - 1))
    def _():
        sum_ref[...] += part

    @pl.when(step == COLUMN_TILES - 1)
    def _():
        total = (sum_ref[...] + part).astype(jnp.bfloat16)
        grad0_ref[...] = total[:length]
        grad1_ref[...] = total[length:]

    branch = f32_dot(jnp.concatenate([m0_ref[...], m1_ref[...]], axis=0), weight)
    branch = branch.astype(jnp.bfloat16)
    branch0_ref[...] = branch[:length]
    branch1_ref[...] = branch[length:]


def project(grad_own, grad_peer, mixed_own, mixed_peer, pieces):
    length, width = grad_own.shape
    half = mixed_own.shape[1]
    tile = width // COLUMN_TILES
    part = pl.BlockSpec((length, tile), lambda j: (0, j))
    whole = pl.BlockSpec((length, half), lambda j: (0, 0))
    return pl.pallas_call(
        project_kernel,
        grid=(COLUMN_TILES,),
        in_specs=[part, part, whole, whole]
        + [pl.BlockSpec((HEAD_DIM, tile), lambda j: (0, j))] * len(pieces),
        out_specs=[whole, whole, part, part],
        out_shape=[jax.ShapeDtypeStruct((length, half), jnp.bfloat16)] * 2
        + [jax.ShapeDtypeStruct((length, width), jnp.bfloat16)] * 2,
        scratch_shapes=[pltpu.VMEM((2 * length, half), jnp.float32)],
        compiler_params=params(),
        cost_estimate=cost(11, 14 * 2**20),
        name="project",
    )(grad_own, grad_peer, mixed_own, mixed_peer, *pieces)


def update_kernel(steps_ref, anchor_ref, local_ref, anchor_out_ref, merged_ref):
    for start in range(0, anchor_ref.shape[1], HEAD_DIM):
        columns = pl.ds(start, HEAD_DIM)
        step = steps_ref[columns, :].astype(jnp.float32).T
        anchor_new = anchor_ref[:, columns] - outer_rate * step
        anchor_out_ref[:, columns] = anchor_new
        merged = mix_factor * local_ref[:, columns].astype(jnp.float32) + mix_factor * anchor_new
        merged_ref[:, columns] = merged.astype(jnp.bfloat16)


def shift(dz, dx, dcore):
    pairs = []
    for z in range(Z_SIZE):
        for x in range(X_SIZE):
            for core in range(2):
                target = ((z + dz) % Z_SIZE) * X_SIZE + (x + dx) % X_SIZE
                pairs.append(((z * X_SIZE + x) * 2 + core, target * 2 + (core + dcore) % 2))
    return pairs


def to_right(array):
    return lax.ppermute(array, "fsdp", shift(0, 1, 0))


def to_left(array):
    return lax.ppermute(array, "fsdp", shift(0, -1, 0))


def to_far(array):
    return lax.ppermute(array, "fsdp", shift(1, 0, 0))


def to_peer(array):
    return lax.ppermute(array, "fsdp", shift(0, 0, 1))


def added(*terms):
    total = terms[0].astype(jnp.float32)
    for term in terms[1:]:
        total = total + term.astype(jnp.float32)
    return total.astype(jnp.bfloat16)


def place_table():
    position = lax.axis_index("fsdp")
    z, x, core = position // (2 * X_SIZE), (position // 2) % X_SIZE, position % 2
    slot_z, slot_x = jnp.array(SLOT_Z, jnp.int32), jnp.array(SLOT_X, jnp.int32)
    heads = ((z + slot_z) % Z_SIZE) * X_SIZE + (x + slot_x) % X_SIZE
    return jnp.concatenate([heads, core[None]]).astype(jnp.int32)


def packed_shares(own_delta):
    rows, replicas = own_delta.shape[0], lax.axis_size("rep")
    shares = own_delta.astype(jnp.bfloat16).reshape(rows, replicas, -1)
    return shares.transpose(1, 2, 0)


def outer_share(packed, momentum):
    replicas = lax.axis_size("rep")
    shares = lax.all_to_all(packed, "rep", 0, 0, tiled=False)
    mean_share = jnp.sum(shares.astype(jnp.float32), axis=0).T / replicas
    momentum_new = outer_moment * momentum + mean_share
    step_share = (outer_moment * momentum_new + mean_share).astype(jnp.bfloat16).T
    return momentum_new, jnp.broadcast_to(step_share[None], (replicas, *step_share.shape))


def outer_update(steps, anchor, local):
    rows, width = anchor.shape
    tile = width // COLUMN_TILES
    steps = lax.all_to_all(steps, "rep", 0, 0, tiled=False).reshape(width, rows)
    part = pl.BlockSpec((rows, tile), lambda j: (0, j))
    return pl.pallas_call(
        update_kernel,
        grid=(COLUMN_TILES,),
        in_specs=[pl.BlockSpec((tile, rows), lambda j: (j, 0)), part, part],
        out_specs=[part, part],
        out_shape=[
            jax.ShapeDtypeStruct(anchor.shape, jnp.float32),
            jax.ShapeDtypeStruct(local.shape, jnp.bfloat16),
        ],
        compiler_params=params(),
        cost_estimate=cost(3, 4 * 2**20),
        name="outer_update",
    )(steps, anchor, local)


def on_device(
    query_states,
    key_states,
    value_states,
    output_grad,
    out_weight,
    pseudo_grad,
    anchor,
    momentum,
    local_weight,
):
    place = place_table()
    own_rows = out_weight[0]
    grad_peer = to_peer(output_grad)

    w3 = to_right(own_rows)
    w1 = to_left(own_rows)
    w4 = to_far(own_rows)
    mixed_own, mixed_other = forward(place, query_states, key_states, value_states)
    mixed_peer = to_peer(mixed_other)
    w1, w3, w4, mixed_own = lax.optimization_barrier((w1, w3, w4, mixed_own))
    w2 = to_right(w3)
    w5 = to_left(w4)
    w7 = to_right(w4)

    d0, d1, d3, d4, d5, d2, d7, d6 = weight_grad_pieces(
        mixed_own, mixed_peer, output_grad, grad_peer
    )
    w5, w2, d6 = lax.optimization_barrier((w5, w2, d6))
    w6 = to_left(w5)
    r2 = to_far(d6)
    r1f = to_far(d5)
    w6, d7 = lax.optimization_barrier((w6, d7))
    r4 = to_left(d7)
    d0, pseudo_grad = lax.optimization_barrier((d0, pseudo_grad))
    momentum_new, steps = outer_share(packed_shares(pseudo_grad[0]), momentum)
    w7, d2 = lax.optimization_barrier((w7, d2))
    s2 = added(d2, r2)
    w6, w7, s2 = lax.optimization_barrier((w6, w7, s2))
    r1 = to_right(s2)
    grad_mixed, grad_send, branch_own, branch_send = project(
        output_grad, grad_peer, mixed_own, mixed_peer, [own_rows, w1, w3, w4, w5, w2, w7, w6]
    )
    s1 = added(d1, r1f, r1)
    s4 = added(d4, r4)
    grad_mixed, s1, s4, steps = lax.optimization_barrier((grad_mixed, s1, s4, steps))
    d3, s4 = lax.optimization_barrier((d3, s4))
    from_right = to_left(d3)
    from_left = to_right(s1)
    from_far = to_far(s4)
    weight_grad = added(d0, from_right, from_left, from_far)[None]
    grad_query, grad_key, grad_value = backward(
        place, query_states, key_states, value_states, grad_mixed, to_peer(grad_send)
    )
    branch_out = added(branch_own, to_peer(branch_send))

    anchor_new, merged = outer_update(steps, anchor, local_weight[0])
    return (
        branch_out,
        grad_query,
        grad_key,
        grad_value,
        weight_grad,
        anchor_new,
        momentum_new,
        merged[None],
    )


def solution(mesh):
    return jax.shard_map(
        on_device,
        mesh=mesh,
        in_specs=(
            P(("rep", "fsdp"), None),
            P(("rep", "fsdp"), None),
            P(("rep", "fsdp"), None),
            P(("rep", "fsdp"), None),
            P("rep", "fsdp", None),
            P("rep", "fsdp", None),
            P("fsdp", None),
            P("fsdp", "rep"),
            P("rep", "fsdp", None),
        ),
        out_specs=(
            P(("rep", "fsdp"), None),
            P(("rep", "fsdp"), None),
            P(("rep", "fsdp"), None),
            P(("rep", "fsdp"), None),
            P("rep", "fsdp", None),
            P("fsdp", None),
            P("fsdp", "rep"),
            P("rep", "fsdp", None),
        ),
        check_vma=False,
    )
```

```python
import math

import jax
import jax.numpy as jnp
from jax import lax
from jax.experimental import pallas as pl
from jax.experimental.pallas import tpu as pltpu
from jax.sharding import PartitionSpec as P

HEADS = 16
KV_HEADS = 8
HEAD_DIM = 128

query_scale = 1.0 / 12.0
outer_rate = 0.7
outer_moment = 0.9
mix_factor = 0.5

X_SIZE = 4
Z_SIZE = 2
VMEM_LIMIT = 56 * 1024 * 1024

NT = (((1,), (1,)), ((), ()))
TN = (((0,), (0,)), ((), ()))


def f32_dot(left, right, dims=(((1,), (0,)), ((), ()))):
    return lax.dot_general(left, right, dims, preferred_element_type=jnp.float32)


def params(**kwargs):
    return pltpu.CompilerParams(vmem_limit_bytes=VMEM_LIMIT, **kwargs)


def cost(microseconds, bytes_accessed):
    return pl.CostEstimate(
        flops=int(microseconds * 2.300e+07), bytes_accessed=bytes_accessed, transcendentals=0
    )


SLOT_Z = (0, 0, 0, 1, 1, 0, 1, 1)
SLOT_X = (0, 1, 3, 0, 1, 2, 3, 2)

ROW_BLOCKS = ((0, 128, 128), (128, 64, 256), (192, 64, 256))


def own_lanes(place_ref, turn):
    parity = place_ref[KV_HEADS] if turn == 0 else 1 - place_ref[KV_HEADS]
    return pl.ds(pl.multiple_of(parity * HEAD_DIM, HEAD_DIM), HEAD_DIM)


def both_heads(place_ref, ref):
    return jnp.concatenate([ref[:, own_lanes(place_ref, turn)] for turn in range(2)], axis=0)


def attention_of(scores):
    def block(turn, first, rows, seen):
        part = scores[pl.ds(turn * scores.shape[1] + first, rows), :seen]
        allowed = first + lax.broadcasted_iota(
            jnp.int32, (rows, seen), 0
        ) >= lax.broadcasted_iota(jnp.int32, (rows, seen), 1)
        part = jnp.where(allowed, part, -jnp.inf)
        highest = jnp.max(part, axis=-1, keepdims=True)
        terms = jnp.exp2((part - highest) * (query_scale * math.log2(math.e)))
        return terms * (1.0 / jnp.sum(terms, axis=-1, keepdims=True))

    return block


def put_rounded(ref, turn, first, rows, seen, values):
    length = ref.shape[1]
    stacked = pl.ds(turn * length + first, rows)
    ref[stacked, :seen] = values.astype(jnp.bfloat16)
    if seen < length:
        ref[stacked, seen:] = jnp.zeros((rows, length - seen), jnp.bfloat16)


def forward_kernel(place_ref, q_ref, k_ref, v_ref, own_ref, other_ref, scores_ref, rounded_ref):
    length = q_ref.shape[0]
    scores_ref[...] = f32_dot(both_heads(place_ref, q_ref), k_ref[...], NT)
    attention = attention_of(scores_ref)
    for turn in range(2):
        for block in ROW_BLOCKS:
            put_rounded(rounded_ref, turn, *block, attention(turn, *block))
    mixed = f32_dot(rounded_ref[...], v_ref[...]).astype(jnp.bfloat16)
    own_ref[...] = mixed[:length]
    other_ref[...] = mixed[length:]


def slot_specs(length):
    return (
        pl.BlockSpec((length, 2 * HEAD_DIM), lambda r, place: (0, place[r])),
        pl.BlockSpec((length, HEAD_DIM), lambda r, place: (0, place[r])),
        pl.BlockSpec((length, HEAD_DIM), lambda r, place: (0, r)),
    )


def forward(place, query_states, key_states, value_states):
    length = query_states.shape[0]
    pair_spec, kv_spec, slot_spec = slot_specs(length)
    out = jax.ShapeDtypeStruct((length, KV_HEADS * HEAD_DIM), jnp.bfloat16)
    return pl.pallas_call(
        forward_kernel,
        grid_spec=pltpu.PrefetchScalarGridSpec(
            num_scalar_prefetch=1,
            grid=(KV_HEADS,),
            in_specs=[pair_spec, kv_spec, kv_spec],
            out_specs=[slot_spec, slot_spec],
            scratch_shapes=[
                pltpu.VMEM((2 * length, length), jnp.float32),
                pltpu.VMEM((2 * length, length), jnp.bfloat16),
            ],
        ),
        out_shape=[out, out],
        compiler_params=params(),
        cost_estimate=cost(7, 4 * 2**20),
        name="attention_forward",
    )(place, query_states, key_states, value_states)


def backward_kernel(place_ref, q_ref, k_ref, v_ref, own_ref, other_ref, *refs):
    dq_ref, dk_ref, dv_ref, scores_ref, probs_ref, grad_scores_ref, rounded_ref = refs
    length = q_ref.shape[0]
    queries = both_heads(place_ref, q_ref)
    grad_mixed = jnp.concatenate([own_ref[...], other_ref[...]], axis=0)
    scores_ref[...] = f32_dot(queries, k_ref[...], NT)
    probs_ref[...] = f32_dot(grad_mixed, v_ref[...], NT)
    attention_block = attention_of(scores_ref)
    for turn in range(2):
        for block in ROW_BLOCKS:
            first, rows, seen = block
            attention = attention_block(turn, *block)
            grad_probs = probs_ref[pl.ds(turn * length + first, rows), :seen]
            row_term = jnp.sum(attention * grad_probs, axis=-1, keepdims=True)
            grad_scores = attention * (grad_probs - row_term) * query_scale
            put_rounded(grad_scores_ref, turn, *block, grad_scores)
            put_rounded(rounded_ref, turn, *block, attention)
    dv_ref[...] = f32_dot(rounded_ref[...], grad_mixed, TN).astype(jnp.bfloat16)
    dk_ref[...] = f32_dot(grad_scores_ref[...], queries, TN).astype(jnp.bfloat16)
    dq = f32_dot(grad_scores_ref[...], k_ref[...]).astype(jnp.bfloat16)
    for turn in range(2):
        dq_ref[:, own_lanes(place_ref, turn)] = dq[turn * length : (turn + 1) * length]


def backward(place, query_states, key_states, value_states, grad_own, grad_other):
    length = query_states.shape[0]
    pair_spec, kv_spec, slot_spec = slot_specs(length)
    return pl.pallas_call(
        backward_kernel,
        grid_spec=pltpu.PrefetchScalarGridSpec(
            num_scalar_prefetch=1,
            grid=(KV_HEADS,),
            in_specs=[pair_spec, kv_spec, kv_spec, slot_spec, slot_spec],
            out_specs=[pair_spec, kv_spec, kv_spec],
            scratch_shapes=[
                pltpu.VMEM((2 * length, length), jnp.float32),
                pltpu.VMEM((2 * length, length), jnp.float32),
                pltpu.VMEM((2 * length, length), jnp.bfloat16),
                pltpu.VMEM((2 * length, length), jnp.bfloat16),
            ],
        ),
        out_shape=[
            jax.ShapeDtypeStruct(query_states.shape, jnp.bfloat16),
            jax.ShapeDtypeStruct(key_states.shape, jnp.bfloat16),
            jax.ShapeDtypeStruct(value_states.shape, jnp.bfloat16),
        ],
        compiler_params=params(),
        cost_estimate=cost(10, 9 * 2**20),
        name="attention_backward",
    )(place, query_states, key_states, value_states, grad_own, grad_other)


COLUMN_TILES = 3


def weight_grad_kernel(m0_ref, m1_ref, g0_ref, g1_ref, *refs):
    *out_refs, mixed_ref = refs
    length = m0_ref.shape[0]

    @pl.when(pl.program_id(0) == 0)
    def _():
        mixed_ref[:, :length] = m0_ref[...].T
        mixed_ref[:, length:] = m1_ref[...].T

    grads = jnp.concatenate([g0_ref[...], g1_ref[...]], axis=0)
    product = f32_dot(mixed_ref[...], grads).astype(jnp.bfloat16)
    for slot, out_ref in enumerate(out_refs):
        out_ref[...] = product[slot * HEAD_DIM : (slot + 1) * HEAD_DIM]


def weight_grad_pieces(mixed_own, mixed_peer, grad_own, grad_peer):
    length, half = mixed_own.shape
    width = grad_own.shape[1]
    tile = width // COLUMN_TILES
    whole = pl.BlockSpec((length, half), lambda j: (0, 0))
    part = pl.BlockSpec((length, tile), lambda j: (0, j))
    return pl.pallas_call(
        weight_grad_kernel,
        grid=(COLUMN_TILES,),
        in_specs=[whole, whole, part, part],
        out_specs=[pl.BlockSpec((HEAD_DIM, tile), lambda j: (0, j))] * KV_HEADS,
        out_shape=[jax.ShapeDtypeStruct((HEAD_DIM, width), jnp.bfloat16)] * KV_HEADS,
        scratch_shapes=[pltpu.VMEM((half, 2 * length), jnp.bfloat16)],
        compiler_params=params(),
        cost_estimate=cost(5, 8 * 2**20),
        name="weight_grad_partial",
    )(mixed_own, mixed_peer, grad_own, grad_peer)


def project_kernel(g0_ref, g1_ref, m0_ref, m1_ref, *refs):
    *pieces, grad0_ref, grad1_ref, branch0_ref, branch1_ref, sum_ref = refs
    step = pl.program_id(0)
    length = g0_ref.shape[0]
    weight = jnp.concatenate([piece[...] for piece in pieces], axis=0)
    part = f32_dot(jnp.concatenate([g0_ref[...], g1_ref[...]], axis=0), weight, NT)

    @pl.when(step == 0)
    def _():
        sum_ref[...] = part

    @pl.when((step > 0) & (step < COLUMN_TILES - 1))
    def _():
        sum_ref[...] += part

    @pl.when(step == COLUMN_TILES - 1)
    def _():
        total = (sum_ref[...] + part).astype(jnp.bfloat16)
        grad0_ref[...] = total[:length]
        grad1_ref[...] = total[length:]

    branch = f32_dot(jnp.concatenate([m0_ref[...], m1_ref[...]], axis=0), weight)
    branch = branch.astype(jnp.bfloat16)
    branch0_ref[...] = branch[:length]
    branch1_ref[...] = branch[length:]


def project(grad_own, grad_peer, mixed_own, mixed_peer, pieces):
    length, width = grad_own.shape
    half = mixed_own.shape[1]
    tile = width // COLUMN_TILES
    part = pl.BlockSpec((length, tile), lambda j: (0, j))
    whole = pl.BlockSpec((length, half), lambda j: (0, 0))
    return pl.pallas_call(
        project_kernel,
        grid=(COLUMN_TILES,),
        in_specs=[part, part, whole, whole]
        + [pl.BlockSpec((HEAD_DIM, tile), lambda j: (0, j))] * len(pieces),
        out_specs=[whole, whole, part, part],
        out_shape=[jax.ShapeDtypeStruct((length, half), jnp.bfloat16)] * 2
        + [jax.ShapeDtypeStruct((length, width), jnp.bfloat16)] * 2,
        scratch_shapes=[pltpu.VMEM((2 * length, half), jnp.float32)],
        compiler_params=params(),
        cost_estimate=cost(11, 14 * 2**20),
        name="project",
    )(grad_own, grad_peer, mixed_own, mixed_peer, *pieces)


def update_kernel(steps_ref, anchor_ref, local_ref, anchor_out_ref, merged_ref):
    for start in range(0, anchor_ref.shape[1], HEAD_DIM):
        columns = pl.ds(start, HEAD_DIM)
        step = steps_ref[columns, :].astype(jnp.float32).T
        anchor_new = anchor_ref[:, columns] - outer_rate * step
        anchor_out_ref[:, columns] = anchor_new
        merged = mix_factor * local_ref[:, columns].astype(jnp.float32) + mix_factor * anchor_new
        merged_ref[:, columns] = merged.astype(jnp.bfloat16)


def shift(dz, dx, dcore):
    pairs = []
    for z in range(Z_SIZE):
        for x in range(X_SIZE):
            for core in range(2):
                target = ((z + dz) % Z_SIZE) * X_SIZE + (x + dx) % X_SIZE
                pairs.append(((z * X_SIZE + x) * 2 + core, target * 2 + (core + dcore) % 2))
    return pairs


def to_right(array):
    return lax.ppermute(array, "fsdp", shift(0, 1, 0))


def to_left(array):
    return lax.ppermute(array, "fsdp", shift(0, -1, 0))


def to_far(array):
    return lax.ppermute(array, "fsdp", shift(1, 0, 0))


def to_peer(array):
    return lax.ppermute(array, "fsdp", shift(0, 0, 1))


def added(*terms):
    total = terms[0].astype(jnp.float32)
    for term in terms[1:]:
        total = total + term.astype(jnp.float32)
    return total.astype(jnp.bfloat16)


def place_table():
    position = lax.axis_index("fsdp")
    z, x, core = position // (2 * X_SIZE), (position // 2) % X_SIZE, position % 2
    slot_z, slot_x = jnp.array(SLOT_Z, jnp.int32), jnp.array(SLOT_X, jnp.int32)
    heads = ((z + slot_z) % Z_SIZE) * X_SIZE + (x + slot_x) % X_SIZE
    return jnp.concatenate([heads, core[None]]).astype(jnp.int32)


def packed_shares(own_delta):
    rows, replicas = own_delta.shape[0], lax.axis_size("rep")
    shares = own_delta.astype(jnp.bfloat16).reshape(rows, replicas, -1)
    return shares.transpose(1, 2, 0)


def outer_share(shares, momentum):
    replicas = lax.axis_size("rep")
    mean_share = jnp.sum(shares.astype(jnp.float32), axis=0).T / replicas
    momentum_new = outer_moment * momentum + mean_share
    step_share = (outer_moment * momentum_new + mean_share).astype(jnp.bfloat16).T
    return momentum_new, jnp.broadcast_to(step_share[None], (replicas, *step_share.shape))


def outer_update(steps, anchor, local):
    rows, width = anchor.shape
    tile = width // COLUMN_TILES
    steps = steps.reshape(width, rows)
    part = pl.BlockSpec((rows, tile), lambda j: (0, j))
    return pl.pallas_call(
        update_kernel,
        grid=(COLUMN_TILES,),
        in_specs=[pl.BlockSpec((tile, rows), lambda j: (j, 0)), part, part],
        out_specs=[part, part],
        out_shape=[
            jax.ShapeDtypeStruct(anchor.shape, jnp.float32),
            jax.ShapeDtypeStruct(local.shape, jnp.bfloat16),
        ],
        compiler_params=params(),
        cost_estimate=cost(3, 4 * 2**20),
        name="outer_update",
    )(steps, anchor, local)


def on_device(
    query_states,
    key_states,
    value_states,
    output_grad,
    out_weight,
    pseudo_grad,
    anchor,
    momentum,
    local_weight,
):
    place = place_table()
    own_rows = out_weight[0]
    grad_peer = to_peer(output_grad)

    w3 = to_right(own_rows)
    w1 = to_left(own_rows)
    w4 = to_far(own_rows)
    packed = packed_shares(pseudo_grad[0])
    query_states, packed = lax.optimization_barrier((query_states, packed))
    shares = lax.all_to_all(packed, "rep", 0, 0, tiled=False)
    mixed_own, mixed_other = forward(place, query_states, key_states, value_states)
    mixed_peer = to_peer(mixed_other)
    w1, w3, w4, mixed_own = lax.optimization_barrier((w1, w3, w4, mixed_own))
    w2 = to_right(w3)
    w5 = to_left(w4)
    w7 = to_right(w4)

    d0, d1, d3, d4, d5, d2, d7, d6 = weight_grad_pieces(
        mixed_own, mixed_peer, output_grad, grad_peer
    )
    w5, w2, d6, shares = lax.optimization_barrier((w5, w2, d6, shares))
    w6 = to_left(w5)
    r2 = to_far(d6)
    r1f = to_far(d5)
    w6, d7 = lax.optimization_barrier((w6, d7))
    r4 = to_left(d7)
    momentum_new, steps = outer_share(shares, momentum)
    w7, d2, _ = lax.optimization_barrier((w7, d2, steps))
    s2 = added(d2, r2)
    w6, w7, s2 = lax.optimization_barrier((w6, w7, s2))
    r1 = to_right(s2)
    grad_mixed, grad_send, branch_own, branch_send = project(
        output_grad, grad_peer, mixed_own, mixed_peer, [own_rows, w1, w3, w4, w5, w2, w7, w6]
    )
    s1 = added(d1, r1f, r1)
    s4 = added(d4, r4)
    grad_mixed, s1, s4 = lax.optimization_barrier((grad_mixed, s1, s4))
    d3, s4 = lax.optimization_barrier((d3, s4))
    from_right = to_left(d3)
    from_left = to_right(s1)
    from_far = to_far(s4)
    weight_grad = added(d0, from_right, from_left, from_far)[None]
    steps = lax.all_to_all(steps, "rep", 0, 0, tiled=False)
    grad_mixed, steps = lax.optimization_barrier((grad_mixed, steps))
    grad_query, grad_key, grad_value = backward(
        place, query_states, key_states, value_states, grad_mixed, to_peer(grad_send)
    )
    branch_out = added(branch_own, to_peer(branch_send))

    anchor_new, merged = outer_update(steps, anchor, local_weight[0])
    return (
        branch_out,
        grad_query,
        grad_key,
        grad_value,
        weight_grad,
        anchor_new,
        momentum_new,
        merged[None],
    )


def solution(mesh):
    return jax.shard_map(
        on_device,
        mesh=mesh,
        in_specs=(
            P(("rep", "fsdp"), None),
            P(("rep", "fsdp"), None),
            P(("rep", "fsdp"), None),
            P(("rep", "fsdp"), None),
            P("rep", "fsdp", None),
            P("rep", "fsdp", None),
            P("fsdp", None),
            P("fsdp", "rep"),
            P("rep", "fsdp", None),
        ),
        out_specs=(
            P(("rep", "fsdp"), None),
            P(("rep", "fsdp"), None),
            P(("rep", "fsdp"), None),
            P(("rep", "fsdp"), None),
            P("rep", "fsdp", None),
            P("fsdp", None),
            P("fsdp", "rep"),
            P("rep", "fsdp", None),
        ),
        check_vma=False,
    )
```
